128 devices in a mesh: sens: 4 (over y_hi, core), par: 32 (over y_lo, z, x).
Axes of the slice: x: 4, y: 4 (y_hi: 2, y_lo: 2; y = y_hi * 2 + y_lo), z: 4, core: 2. Of those that a mesh axis runs over, the one named last changes fastest.
Arguments:
- probes: float32 [2048, 512], P('par', 'sens'), may hold values from -6 to 6
- kernel: float32 [64, 2048, 2048], P(None, 'par', 'sens'), may hold values from -0.015625 to 0.015625
- noise_inverse: float32 [64, 64], replicated, may hold values from -1 to 3, as said below
- sensor_weight: float32 [2048], P('sens'), may hold values from 0.25 to 4
Outputs:
- hessian_action: float32 [2048, 512], P('par', 'sens')
The draws below stay inside these ranges and needn't reach their ends.
Inputs may be any that keep to these rules, and one draw needn't show every extreme that they name: `noise_inverse`: symmetric.
All inputs are finite; a program needn't handle non-finite values.
Results may differ from the reference program's by a relative error of at most 0.0001.
Values sent between devices are 32-bit elements; how exact they have to be, the bound alone decides.
No kernel may reach another device: no remote copies, remote signals or barrier semaphores. Data moves between devices by JAX's collectives and lax.ppermute only.
A program may use at most 128 MiB of HBM per device.

```python
import math
import jax
import jax.numpy as jnp
from jax import lax

NS = 2048
NP = 2048
NT = 64
PROBES = 8


def draw_noise_inverse(key, part):
    first, second = jax.random.split(jax.random.fold_in(key, 17))
    offdiag = jnp.clip(jax.random.normal(first, (NT, NT), jnp.float32), -4.0, 4.0)
    offdiag = (offdiag + offdiag.T) * (0.12 / NT ** 0.5)
    diagonal = jax.random.uniform(second, (NT,), jnp.float32, 1.0, 2.0)
    return offdiag + jnp.diag(diagonal)


def level_of(stream_key, shape, cuts, low, top_value):
    loudness = 1.0
    for dim, parts in cuts:
        heights = jax.random.uniform(jax.random.fold_in(jax.random.fold_in(stream_key, 6), dim), (parts,), jnp.float32, low / len(cuts), top_value / len(cuts))
        loudness = loudness * jnp.repeat(jnp.exp(heights), shape[dim] // parts).reshape((-1,) + (1,) * (len(shape) - 1 - dim))
    return loudness


def normal_values(rng, dims, deviation, limit, cuts=(), kind=jnp.bfloat16):
    values = jax.random.normal(rng, dims, jnp.float32) * deviation
    if len(cuts) > 0:
        values = level_of(rng, dims, cuts, -0.22, 0.18) * values
    return jnp.clip(values, min=-limit, max=limit).astype(kind)


def setup_inputs(seed: int = 0) -> dict:
    streams_of = jax.random.split(jax.random.key(seed), 5)
    probes = normal_values(streams_of[0], (NP, NT * PROBES), 1.0, 6.0, ((0, 32), (1, 4)), jnp.float32)
    kernel = normal_values(streams_of[1], (NT, NP, NS), (NP * NT) ** -0.5, 0.015625, ((1, 32), (2, 4)), jnp.float32)
    noise_inverse = draw_noise_inverse(jax.random.fold_in(streams_of[4], 71), 0)
    sensor_weight = jnp.clip(jnp.exp(math.log(4.0) - 2.7725887 * jax.random.uniform(streams_of[3], (NS,), jnp.float32) ** level_of(streams_of[3], (NS,), ((0, 4),), -0.2, 0.2)), 0.25, 4.0)
    return dict(probes=probes, kernel=kernel, noise_inverse=noise_inverse, sensor_weight=sensor_weight)


def shift_later(field, lag_index):
    padded = jnp.pad(field, ((0, 0), (NT, 0), (0, 0)))
    return lax.dynamic_slice_in_dim(padded, NT - lag_index, NT, 1)


def shift_earlier(field, lag_index):
    padded = jnp.pad(field, ((0, 0), (0, NT), (0, 0)))
    return lax.dynamic_slice_in_dim(padded, lag_index, NT, 1)


def reference(probes, kernel, noise_inverse, sensor_weight):
    highest = lax.Precision.HIGHEST
    probe_field = probes.reshape(NP, NT, PROBES)
    lag_list = jnp.arange(NT, dtype=jnp.int32)

    def forward(running, lag_index):
        kernel_lag = lax.dynamic_index_in_dim(kernel, lag_index, 0, keepdims=False)
        moved = shift_later(probe_field, lag_index).reshape(NP, NT * PROBES)
        term = lax.dot_general(kernel_lag, moved, (((0,), (0,)), ((), ())), precision=highest, preferred_element_type=jnp.float32)
        return running + term, None

    observed, _ = lax.scan(forward, jnp.zeros((NS, NT * PROBES), jnp.float32), lag_list)
    mixed = jnp.einsum("tu,rup->rtp", noise_inverse, observed.reshape(NS, NT, PROBES), precision=highest, preferred_element_type=jnp.float32)
    weighted = mixed.reshape(NS, NT * PROBES) * sensor_weight[:, None]

    def backward(running, lag_index):
        kernel_lag = lax.dynamic_index_in_dim(kernel, lag_index, 0, keepdims=False)
        spread = jnp.dot(kernel_lag, weighted, precision=highest, preferred_element_type=jnp.float32).reshape(NP, NT, PROBES)
        return running + shift_earlier(spread, lag_index), None

    result, _ = lax.scan(backward, jnp.zeros((NP, NT, PROBES), jnp.float32), lag_list)
    return result.reshape(NP, NT * PROBES)
```

```python
import jax
import jax.numpy as jnp
from jax import lax
from jax.experimental import pallas as pl
from jax.experimental.pallas import tpu as pltpu
from jax.sharding import PartitionSpec as P

F32 = jnp.float32
BF16 = jnp.bfloat16
GROUP = 4
TIERS = 4


def split(value):
    high = value.astype(BF16)
    return high, (value - high.astype(F32)).astype(BF16)


def kernel_copies(kernel_ref, held, sems, block_rows, blocks):
    return [
        pltpu.make_async_copy(
            kernel_ref.at[pl.ds(b * block_rows, block_rows)],
            held.at[pl.ds(b * block_rows, block_rows)],
            sems.at[b],
        )
        for b in range(blocks)
    ]


def wait_block(kernel_ref, held, sems, block_rows, b):
    rows = pl.ds(pl.multiple_of(b * block_rows, block_rows), block_rows)
    pltpu.make_async_copy(kernel_ref.at[rows], held.at[rows], sems.at[b]).wait()
    return rows


def forward_kernel(p0, p1, p2, p3, kernel_ref, out_ref, held, field, moved, sems):
    params, part_columns = p0.shape
    columns = out_ref.shape[0]
    block_rows = GROUP * params
    blocks = kernel_ref.shape[0] // block_rows
    step_rows = 8 * GROUP
    per_tier = blocks // TIERS
    tier_rows = columns // TIERS
    pad = tier_rows - step_rows
    for copy in kernel_copies(kernel_ref, held, sems, block_rows, blocks):
        copy.start()
    me = lax.axis_index("sens")
    field[pl.ds(0, step_rows), :] = jnp.zeros((step_rows, params), F32)
    for other, piece in enumerate((p0, p1, p2, p3)):
        start = step_rows + part_columns * jnp.bitwise_xor(me, other)
        field[pl.ds(pl.multiple_of(start, step_rows), part_columns), :] = piece[...].T
    shifted = jnp.concatenate(
        [field[pl.ds(step_rows - 8 * lag, columns), :] for lag in range(GROUP)], axis=1
    )
    high, low = split(shifted)
    moved[pl.ds(0, pad), :] = jnp.zeros((pad, 3 * block_rows), BF16)
    moved[pl.ds(pad, columns), pl.ds(0, block_rows)] = high
    moved[pl.ds(pad, columns), pl.ds(block_rows, block_rows)] = high
    moved[pl.ds(pad, columns), pl.ds(2 * block_rows, block_rows)] = low
    out_ref[...] = jnp.zeros_like(out_ref)
    for tier in range(TIERS):
        first = tier * tier_rows
        count = columns - first

        @pl.loop(0, per_tier)
        def _(i, tier=tier, first=first, count=count):
            rows = wait_block(kernel_ref, held, sems, block_rows, tier * per_tier + i)
            k_high, k_low = split(held[rows, :])
            weights = jnp.concatenate([k_high, k_low, k_high], axis=0)
            start = pl.multiple_of(pad - step_rows * i, step_rows)
            out_ref[pl.ds(first, count), :] += jnp.dot(
                moved[pl.ds(start, count), :], weights, preferred_element_type=F32
            )


def backward_kernel(
    observed, noise, sensor_weight, kernel_ref, kept, sent, held, spread, weighted, sems
):
    columns, sensors = observed.shape
    params = kept.shape[1]
    part_columns = kept.shape[2]
    time_steps = noise.shape[0]
    block_rows = GROUP * params
    blocks = kernel_ref.shape[0] // block_rows
    step_rows = 8 * GROUP
    per_tier = blocks // TIERS
    tier_rows = columns // TIERS
    pad = tier_rows - step_rows
    for copy in kernel_copies(kernel_ref, held, sems, block_rows, blocks):
        copy.start()

    row = lax.broadcasted_iota(jnp.int32, (time_steps, columns), 0)
    col = lax.broadcasted_iota(jnp.int32, (time_steps, columns), 1)
    expand = jnp.where(row == col // 8, 1.0, 0.0).astype(BF16)
    same = (
        lax.broadcasted_iota(jnp.int32, (1, 8, columns), 1)
        == lax.broadcasted_iota(jnp.int32, (1, 8, columns), 2) % 8
    )

    def widen(part):
        wide = jnp.dot(part, expand, preferred_element_type=F32)
        wide = jnp.where(same, wide[:, None, :], 0.0)
        return wide.reshape(columns, columns).astype(BF16)

    n_high, n_low = [widen(part) for part in split(noise[...])]
    o_high, o_low = split(observed[...])
    mixed = jnp.dot(n_high, o_high, preferred_element_type=F32)
    mixed += jnp.dot(n_high, o_low, preferred_element_type=F32)
    mixed += jnp.dot(n_low, o_high, preferred_element_type=F32)
    high, low = split(mixed * sensor_weight[...])
    weighted[pl.ds(0, columns), pl.ds(0, sensors)] = high
    weighted[pl.ds(0, columns), pl.ds(sensors, sensors)] = high
    weighted[pl.ds(0, columns), pl.ds(2 * sensors, sensors)] = low
    weighted[pl.ds(columns, pad), :] = jnp.zeros((pad, 3 * sensors), BF16)
    spread[...] = jnp.zeros_like(spread)
    for tier in range(TIERS):
        first = tier * tier_rows
        count = columns - first

        @pl.loop(0, per_tier)
        def _(i, tier=tier, first=first, count=count):
            rows = wait_block(kernel_ref, held, sems, block_rows, tier * per_tier + i)
            k_high, k_low = split(held[rows, :])
            weights = jnp.concatenate([k_high, k_low, k_high], axis=1)
            start = pl.multiple_of(first + step_rows * i, step_rows)
            spread[pl.ds(0, count), :] += lax.dot_general(
                weighted[pl.ds(start, count), :],
                weights,
                (((1,), (1,)), ((), ())),
                preferred_element_type=F32,
            )

    me = lax.axis_index("sens")
    for other, target in enumerate((kept.at[0], sent.at[0], kept.at[1], sent.at[1])):
        start = pl.multiple_of(part_columns * jnp.bitwise_xor(me, other), part_columns)
        total = spread[pl.ds(start, part_columns), pl.ds(0, params)]
        for lag in range(1, GROUP):
            total += spread[pl.ds(start + 8 * lag, part_columns), pl.ds(lag * params, params)]
        target[...] = total.T


def per_device(probes, kernel, noise_inverse, sensor_weight):
    time_steps, params, sensors = kernel.shape
    part_columns = probes.shape[1]
    ranks = lax.axis_size("sens")
    columns = part_columns * ranks
    blocks = time_steps // GROUP
    block_rows = GROUP * params
    par = lax.axis_size("par")
    swap_core = [(s, s ^ 1) for s in range(ranks)]
    swap_chip = [(s, s ^ 2) for s in range(ranks)]
    kernel_flat = kernel.reshape(time_steps * params, sensors)
    vmem = pl.BlockSpec(memory_space=pltpu.VMEM)
    anywhere = pl.BlockSpec(memory_space=pl.ANY)
    compiler_params = pltpu.CompilerParams(vmem_limit_bytes=40 * 1024 * 1024)
    step_rows = 8 * GROUP
    pad = columns // TIERS - step_rows

    across = lax.ppermute(probes, "sens", swap_chip)
    beside = lax.ppermute(probes, "sens", swap_core)
    diagonal = lax.ppermute(across, "sens", swap_core)

    partial = pl.pallas_call(
        forward_kernel,
        out_shape=jax.ShapeDtypeStruct((columns, sensors), F32),
        in_specs=[vmem] * 4 + [anywhere],
        out_specs=vmem,
        scratch_shapes=[
            pltpu.VMEM((time_steps * params, sensors), F32),
            pltpu.VMEM((step_rows + columns, params), F32),
            pltpu.VMEM((pad + columns, 3 * block_rows), BF16),
            pltpu.SemaphoreType.DMA((blocks,)),
        ],
        compiler_params=compiler_params,
        name="forward_map",
    )(probes, beside, across, diagonal, kernel_flat)

    pieces = lax.all_to_all(
        partial.reshape(par, columns // par, sensors), "par", 0, 0, tiled=True
    )
    share = jnp.sum(pieces, axis=0)
    observed = lax.all_to_all(
        jnp.broadcast_to(share[None], pieces.shape), "par", 0, 0, tiled=True
    ).reshape(columns, sensors)

    piece = jax.ShapeDtypeStruct((2, params, part_columns), F32)
    kept, sent = pl.pallas_call(
        backward_kernel,
        out_shape=(piece, piece),
        in_specs=[vmem] * 3 + [anywhere],
        out_specs=(vmem, vmem),
        scratch_shapes=[
            pltpu.VMEM((time_steps * params, sensors), F32),
            pltpu.VMEM((columns + step_rows, block_rows), F32),
            pltpu.VMEM((columns + pad, 3 * sensors), BF16),
            pltpu.SemaphoreType.DMA((blocks,)),
        ],
        compiler_params=compiler_params,
        name="backward_map",
    )(observed, noise_inverse, sensor_weight.reshape(1, sensors), kernel_flat)
    kept += lax.ppermute(sent, "sens", swap_core)
    return kept[0] + lax.ppermute(kept[1], "sens", swap_chip)


def solution(mesh):
    placed = (P("par", "sens"), P(None, "par", "sens"), P(), P("sens"))
    return jax.shard_map(
        per_device, mesh=mesh, in_specs=placed, out_specs=P("par", "sens"), check_vma=False
    )
```

```python
import jax
import jax.numpy as jnp
from jax import lax
from jax.experimental import pallas as pl
from jax.experimental.pallas import tpu as pltpu
from jax.sharding import PartitionSpec as P

F32 = jnp.float32
BF16 = jnp.bfloat16
GROUP = 4


def split(value):
    high = value.astype(BF16)
    return high, (value - high.astype(F32)).astype(BF16)


def prepare_kernel(kernel_ref, k_high, k_low, held, sems):
    blocks = sems.shape[0]
    block_rows = held.shape[0] // blocks

    def block_copy(b):
        rows = pl.ds(pl.multiple_of(b * block_rows, block_rows), block_rows)
        return rows, pltpu.make_async_copy(kernel_ref.at[rows], held.at[rows], sems.at[b])

    for b in range(blocks):
        block_copy(b)[1].start()

    @pl.loop(0, blocks)
    def _(b):
        rows, copy = block_copy(b)
        copy.wait()
        high, low = split(held[rows, :])
        k_high[rows, :] = high
        k_low[rows, :] = low


def widen_noise(noise, wide_refs):
    time_steps = noise.shape[0]
    columns = wide_refs[0].shape[0]
    row = lax.broadcasted_iota(jnp.int32, (time_steps, columns), 0)
    col = lax.broadcasted_iota(jnp.int32, (time_steps, columns), 1)
    expand = jnp.where(row == col // 8, 1.0, 0.0).astype(BF16)
    same = (
        lax.broadcasted_iota(jnp.int32, (1, 8, columns), 1)
        == lax.broadcasted_iota(jnp.int32, (1, 8, columns), 2) % 8
    )
    for part, wide_ref in zip(split(noise[...]), wide_refs):
        wide = jnp.dot(part, expand, preferred_element_type=F32)
        wide = jnp.where(same, wide[:, None, :], 0.0)
        wide_ref[...] = wide.reshape(columns, columns).astype(BF16)


def forward_kernel(
    p0, p1, p2, p3, noise, k_high, k_low, out_ref, n_high, n_low, field, f_high, f_low
):
    params, part_columns = p0.shape
    columns = out_ref.shape[0]
    block_rows = GROUP * params
    step_rows = 8 * GROUP
    me = lax.axis_index("sens")
    field[pl.ds(0, step_rows), :] = jnp.zeros((step_rows, params), F32)
    for other, piece in enumerate((p0, p1, p2, p3)):
        start = step_rows + part_columns * jnp.bitwise_xor(me, other)
        field[pl.ds(pl.multiple_of(start, step_rows), part_columns), :] = piece[...].T
    shifted = jnp.concatenate(
        [field[pl.ds(step_rows - 8 * lag, columns), :] for lag in range(GROUP)], axis=1
    )
    f_high[...], f_low[...] = split(shifted)
    widen_noise(noise, (n_high, n_low))
    for b in range(k_high.shape[0] // block_rows):
        rows = pl.ds(b * block_rows, block_rows)
        source = pl.ds(0, columns - step_rows * b)
        target = pl.ds(step_rows * b, columns - step_rows * b)
        term = jnp.dot(f_high[source, :], k_high[rows, :], preferred_element_type=F32)
        term += jnp.dot(f_high[source, :], k_low[rows, :], preferred_element_type=F32)
        term += jnp.dot(f_low[source, :], k_high[rows, :], preferred_element_type=F32)
        if b == 0:
            out_ref[target, :] = term
        else:
            out_ref[target, :] += term


def share_kernel(pieces, k_high, k_low, out_ref):
    del k_high, k_low
    total = jnp.sum(pieces[...], axis=0)
    for part in range(out_ref.shape[0]):
        out_ref[part] = total


def backward_kernel(
    observed, n_high, n_low, sensor_weight, k_high, k_low, kept, sent, spread, weighted
):
    columns, sensors = observed.shape
    params = kept.shape[1]
    part_columns = kept.shape[2]
    block_rows = GROUP * params
    step_rows = 8 * GROUP
    o_high, o_low = split(observed[...])
    mixed = jnp.dot(n_high[...], o_high, preferred_element_type=F32)
    mixed += jnp.dot(n_high[...], o_low, preferred_element_type=F32)
    mixed += jnp.dot(n_low[...], o_high, preferred_element_type=F32)
    high, low = split(mixed * sensor_weight[...])
    weighted[:, pl.ds(0, sensors)] = high
    weighted[:, pl.ds(sensors, sensors)] = high
    weighted[:, pl.ds(2 * sensors, sensors)] = low
    spread[pl.ds(columns, step_rows), :] = jnp.zeros((step_rows, block_rows), F32)
    for b in range(k_high.shape[0] // block_rows):
        rows = pl.ds(b * block_rows, block_rows)
        source = pl.ds(step_rows * b, columns - step_rows * b)
        target = pl.ds(0, columns - step_rows * b)
        weights = jnp.concatenate([k_high[rows, :], k_low[rows, :], k_high[rows, :]], axis=1)
        term = lax.dot_general(
            weighted[source, :], weights, (((1,), (1,)), ((), ())), preferred_element_type=F32
        )
        if b == 0:
            spread[target, :] = term
        else:
            spread[target, :] += term

    me = lax.axis_index("sens")
    for other, target in enumerate((kept.at[0], sent.at[0], kept.at[1], sent.at[1])):
        start = pl.multiple_of(part_columns * jnp.bitwise_xor(me, other), part_columns)
        total = spread[pl.ds(start, part_columns), pl.ds(0, params)]
        for lag in range(1, GROUP):
            total += spread[pl.ds(start + 8 * lag, part_columns), pl.ds(lag * params, params)]
        target[...] = total.T


def per_device(probes, kernel, noise_inverse, sensor_weight):
    time_steps, params, sensors = kernel.shape
    part_columns = probes.shape[1]
    ranks = lax.axis_size("sens")
    columns = part_columns * ranks
    blocks = time_steps // GROUP
    block_rows = GROUP * params
    par = lax.axis_size("par")
    swap_core = [(s, s ^ 1) for s in range(ranks)]
    swap_chip = [(s, s ^ 2) for s in range(ranks)]
    kernel_rows = time_steps * params
    vmem = pl.BlockSpec(memory_space=pltpu.VMEM)
    hbm = pl.BlockSpec(memory_space=pltpu.HBM)
    compiler_params = pltpu.CompilerParams(vmem_limit_bytes=24 * 1024 * 1024)
    step_rows = 8 * GROUP

    across = lax.ppermute(probes, "sens", swap_chip)
    diagonal = lax.ppermute(probes, "sens", [(s, s ^ 3) for s in range(ranks)])
    beside = lax.ppermute(probes, "sens", swap_core)

    half_kernel = jax.ShapeDtypeStruct((kernel_rows, sensors), BF16)
    half_noise = jax.ShapeDtypeStruct((columns, columns), BF16)
    k_high, k_low = pl.pallas_call(
        prepare_kernel,
        out_shape=(half_kernel, half_kernel),
        in_specs=[hbm],
        out_specs=(vmem, vmem),
        scratch_shapes=[
            pltpu.VMEM((kernel_rows, sensors), F32),
            pltpu.SemaphoreType.DMA((blocks,)),
        ],
        compiler_params=pltpu.CompilerParams(vmem_limit_bytes=40 * 1024 * 1024),
        cost_estimate=pl.CostEstimate(
            flops=8 * kernel_rows * sensors,
            bytes_accessed=8 * kernel_rows * sensors,
            transcendentals=0,
        ),
        name="prepare",
    )(kernel.reshape(kernel_rows, sensors))

    partial, n_high, n_low = pl.pallas_call(
        forward_kernel,
        out_shape=(
            jax.ShapeDtypeStruct((columns, sensors), F32),
            half_noise,
            half_noise,
        ),
        in_specs=[vmem] * 7,
        out_specs=(vmem,) * 3,
        scratch_shapes=[
            pltpu.VMEM((step_rows + columns, params), F32),
            pltpu.VMEM((columns, block_rows), BF16),
            pltpu.VMEM((columns, block_rows), BF16),
        ],
        compiler_params=compiler_params,
        name="forward_map",
    )(probes, beside, across, diagonal, noise_inverse, k_high, k_low)

    pieces = lax.all_to_all(
        partial.reshape(par, columns // par, sensors), "par", 0, 0, tiled=True
    )
    shares = pl.pallas_call(
        share_kernel,
        out_shape=jax.ShapeDtypeStruct(pieces.shape, F32),
        in_specs=[vmem] * 3,
        out_specs=vmem,
        compiler_params=compiler_params,
        name="share",
    )(pieces, k_high, k_low)
    observed = lax.all_to_all(shares, "par", 0, 0, tiled=True).reshape(columns, sensors)

    piece = jax.ShapeDtypeStruct((2, params, part_columns), F32)
    kept, sent = pl.pallas_call(
        backward_kernel,
        out_shape=(piece, piece),
        in_specs=[vmem] * 6,
        out_specs=(vmem, vmem),
        scratch_shapes=[
            pltpu.VMEM((columns + step_rows, block_rows), F32),
            pltpu.VMEM((columns, 3 * sensors), BF16),
        ],
        compiler_params=compiler_params,
        name="backward_map",
    )(observed, n_high, n_low, sensor_weight.reshape(1, sensors), k_high, k_low)
    kept += lax.ppermute(sent, "sens", swap_core)
    return kept[0] + lax.ppermute(kept[1], "sens", swap_chip)


def solution(mesh):
    placed = (P("par", "sens"), P(None, "par", "sens"), P(), P("sens"))
    return jax.shard_map(
        per_device, mesh=mesh, in_specs=placed, out_specs=P("par", "sens"), check_vma=False
    )
```

```python
import jax
import jax.numpy as jnp
from jax import lax
from jax.experimental import pallas as pl
from jax.experimental.pallas import tpu as pltpu
from jax.sharding import PartitionSpec as P

F32 = jnp.float32
BF16 = jnp.bfloat16
GROUP = 4
NOISE_ROWS = 128


def split(value):
    high = value.astype(BF16)
    return high, (value - high.astype(F32)).astype(BF16)


def transposed_dot(left, right):
    return lax.dot_general(left, right, (((1,), (1,)), ((), ())), preferred_element_type=F32)


def prepare_kernel(kernel_ref, k_high, k_low, held, sems):
    blocks = sems.shape[0]
    block_rows = held.shape[0] // blocks

    def block_copy(b):
        rows = pl.ds(pl.multiple_of(b * block_rows, block_rows), block_rows)
        return rows, pltpu.make_async_copy(kernel_ref.at[rows], held.at[rows], sems.at[b])

    for b in range(blocks):
        block_copy(b)[1].start()

    @pl.loop(0, blocks)
    def _(b):
        rows, copy = block_copy(b)
        copy.wait()
        high, low = split(held[rows, :])
        k_high[rows, :] = high
        k_low[rows, :] = low


def widen_noise(noise, wide_refs):
    time_steps = noise.shape[0]
    columns = wide_refs[0].shape[0]
    row = lax.broadcasted_iota(jnp.int32, (time_steps, columns), 0)
    col = lax.broadcasted_iota(jnp.int32, (time_steps, columns), 1)
    expand = jnp.where(row == col // 8, 1.0, 0.0).astype(BF16)
    same = (
        lax.broadcasted_iota(jnp.int32, (1, 8, columns), 1)
        == lax.broadcasted_iota(jnp.int32, (1, 8, columns), 2) % 8
    )
    for part, wide_ref in zip(split(noise[...]), wide_refs):
        wide = jnp.dot(part, expand, preferred_element_type=F32)
        wide = jnp.where(same, wide[:, None, :], 0.0)
        wide_ref[...] = wide.reshape(columns, columns).astype(BF16)


def forward_kernel(
    p0, p1, p2, p3, noise, k_high, k_low, out_ref, n_high, n_low, field, f_high, f_low
):
    params, part_columns = p0.shape
    columns = out_ref.shape[0]
    block_rows = GROUP * params
    step_rows = 8 * GROUP
    me = lax.axis_index("sens")
    field[pl.ds(0, step_rows), :] = jnp.zeros((step_rows, params), F32)
    for other, piece in enumerate((p0, p1, p2, p3)):
        start = step_rows + part_columns * jnp.bitwise_xor(me, other)
        field[pl.ds(pl.multiple_of(start, step_rows), part_columns), :] = piece[...].T
    shifted = jnp.concatenate(
        [field[pl.ds(step_rows - 8 * lag, columns), :] for lag in range(GROUP)], axis=1
    )
    f_high[...], f_low[...] = split(shifted)
    widen_noise(noise, (n_high, n_low))
    for b in range(k_high.shape[0] // block_rows):
        rows = pl.ds(b * block_rows, block_rows)
        source = pl.ds(0, columns - step_rows * b)
        target = pl.ds(step_rows * b, columns - step_rows * b)
        term = jnp.dot(f_high[source, :], k_high[rows, :], preferred_element_type=F32)
        term += jnp.dot(f_high[source, :], k_low[rows, :], preferred_element_type=F32)
        term += jnp.dot(f_low[source, :], k_high[rows, :], preferred_element_type=F32)
        if b == 0:
            out_ref[target, :] = term
        else:
            out_ref[target, :] += term


def share_kernel(pieces, k_high, k_low, out_ref):
    del k_high, k_low
    total = jnp.sum(pieces[...], axis=0)
    for part in range(out_ref.shape[0]):
        out_ref[part] = total


def backward_kernel(
    observed, n_high, n_low, sensor_weight, k_high, k_low, kept, sent,
    spread, w_high, w_low, o_high, o_low,
):
    columns, sensors = observed.shape
    params = kept.shape[1]
    part_columns = kept.shape[2]
    block_rows = GROUP * params
    step_rows = 8 * GROUP
    o_high[...], o_low[...] = split(observed[...])
    for start in range(0, columns, NOISE_ROWS):
        rows = pl.ds(start, NOISE_ROWS)
        mixed = jnp.dot(n_high[rows, :], o_high[...], preferred_element_type=F32)
        mixed += jnp.dot(n_high[rows, :], o_low[...], preferred_element_type=F32)
        mixed += jnp.dot(n_low[rows, :], o_high[...], preferred_element_type=F32)
        w_high[rows, :], w_low[rows, :] = split(mixed * sensor_weight[...])
    spread[pl.ds(columns, step_rows), :] = jnp.zeros((step_rows, block_rows), F32)
    for b in range(k_high.shape[0] // block_rows):
        rows = pl.ds(b * block_rows, block_rows)
        source = pl.ds(step_rows * b, columns - step_rows * b)
        target = pl.ds(0, columns - step_rows * b)
        term = transposed_dot(w_high[source, :], k_high[rows, :])
        term += transposed_dot(w_high[source, :], k_low[rows, :])
        term += transposed_dot(w_low[source, :], k_high[rows, :])
        if b == 0:
            spread[target, :] = term
        else:
            spread[target, :] += term

    me = lax.axis_index("sens")
    for other, target in enumerate((kept.at[0], sent.at[0], kept.at[1], sent.at[1])):
        start = pl.multiple_of(part_columns * jnp.bitwise_xor(me, other), part_columns)
        total = spread[pl.ds(start, part_columns), pl.ds(0, params)]
        for lag in range(1, GROUP):
            total += spread[pl.ds(start + 8 * lag, part_columns), pl.ds(lag * params, params)]
        target[...] = total.T


def per_device(probes, kernel, noise_inverse, sensor_weight):
    time_steps, params, sensors = kernel.shape
    part_columns = probes.shape[1]
    ranks = lax.axis_size("sens")
    columns = part_columns * ranks
    blocks = time_steps // GROUP
    block_rows = GROUP * params
    par = lax.axis_size("par")
    swap_core = [(s, s ^ 1) for s in range(ranks)]
    swap_chip = [(s, s ^ 2) for s in range(ranks)]
    kernel_rows = time_steps * params
    vmem = pl.BlockSpec(memory_space=pltpu.VMEM)
    hbm = pl.BlockSpec(memory_space=pltpu.HBM)
    compiler_params = pltpu.CompilerParams(vmem_limit_bytes=24 * 1024 * 1024)
    step_rows = 8 * GROUP

    across = lax.ppermute(probes, "sens", swap_chip)
    diagonal = lax.ppermute(probes, "sens", [(s, s ^ 3) for s in range(ranks)])
    beside = lax.ppermute(probes, "sens", swap_core)

    half_kernel = jax.ShapeDtypeStruct((kernel_rows, sensors), BF16)
    half_noise = jax.ShapeDtypeStruct((columns, columns), BF16)
    k_high, k_low = pl.pallas_call(
        prepare_kernel,
        out_shape=(half_kernel, half_kernel),
        in_specs=[hbm],
        out_specs=(vmem, vmem),
        scratch_shapes=[
            pltpu.VMEM((kernel_rows, sensors), F32),
            pltpu.SemaphoreType.DMA((blocks,)),
        ],
        compiler_params=pltpu.CompilerParams(vmem_limit_bytes=40 * 1024 * 1024),
        cost_estimate=pl.CostEstimate(
            flops=8 * kernel_rows * sensors,
            bytes_accessed=8 * kernel_rows * sensors,
            transcendentals=0,
        ),
        name="prepare",
    )(kernel.reshape(kernel_rows, sensors))

    partial, n_high, n_low = pl.pallas_call(
        forward_kernel,
        out_shape=(
            jax.ShapeDtypeStruct((columns, sensors), F32),
            half_noise,
            half_noise,
        ),
        in_specs=[vmem] * 7,
        out_specs=(vmem,) * 3,
        scratch_shapes=[
            pltpu.VMEM((step_rows + columns, params), F32),
            pltpu.VMEM((columns, block_rows), BF16),
            pltpu.VMEM((columns, block_rows), BF16),
        ],
        compiler_params=compiler_params,
        name="forward_map",
    )(probes, beside, across, diagonal, noise_inverse, k_high, k_low)

    pieces = lax.all_to_all(
        partial.reshape(par, columns // par, sensors), "par", 0, 0, tiled=True
    )
    shares = pl.pallas_call(
        share_kernel,
        out_shape=jax.ShapeDtypeStruct(pieces.shape, F32),
        in_specs=[vmem] * 3,
        out_specs=vmem,
        compiler_params=compiler_params,
        name="share",
    )(pieces, k_high, k_low)
    observed = lax.all_to_all(shares, "par", 0, 0, tiled=True).reshape(columns, sensors)

    piece = jax.ShapeDtypeStruct((2, params, part_columns), F32)
    kept, sent = pl.pallas_call(
        backward_kernel,
        out_shape=(piece, piece),
        in_specs=[vmem] * 6,
        out_specs=(vmem, vmem),
        scratch_shapes=[
            pltpu.VMEM((columns + step_rows, block_rows), F32),
            pltpu.VMEM((columns, sensors), BF16),
            pltpu.VMEM((columns, sensors), BF16),
            pltpu.VMEM((columns, sensors), BF16),
            pltpu.VMEM((columns, sensors), BF16),
        ],
        compiler_params=compiler_params,
        name="backward_map",
    )(observed, n_high, n_low, sensor_weight.reshape(1, sensors), k_high, k_low)
    kept += lax.ppermute(sent, "sens", swap_core)
    return kept[0] + lax.ppermute(kept[1], "sens", swap_chip)


def solution(mesh):
    placed = (P("par", "sens"), P(None, "par", "sens"), P(), P("sens"))
    return jax.shard_map(
        per_device, mesh=mesh, in_specs=placed, out_specs=P("par", "sens"), check_vma=False
    )
```

```python
import jax
import jax.numpy as jnp
from jax import lax
from jax.experimental import pallas as pl
from jax.experimental.pallas import tpu as pltpu
from jax.sharding import PartitionSpec as P

F32 = jnp.float32
BF16 = jnp.bfloat16
GROUP = 4
PIECES = 8
NOISE_ROWS = 128


def split(value):
    high = value.astype(BF16)
    return high, (value - high.astype(F32)).astype(BF16)


def transposed_dot(left, right):
    return lax.dot_general(left, right, (((1,), (1,)), ((), ())), preferred_element_type=F32)


def prepare_kernel(kernel_ref, k_high, k_low, held, sems):
    blocks = sems.shape[0]
    block_rows = held.shape[0] // blocks

    def block_copy(b):
        rows = pl.ds(pl.multiple_of(b * block_rows, block_rows), block_rows)
        return rows, pltpu.make_async_copy(kernel_ref.at[rows], held.at[rows], sems.at[b])

    for b in range(blocks):
        block_copy(b)[1].start()

    @pl.loop(0, blocks)
    def _(b):
        rows, copy = block_copy(b)
        copy.wait()
        high, low = split(held[rows, :])
        k_high[rows, :] = high
        k_low[rows, :] = low


def widen_noise(noise, wide_refs):
    time_steps = noise.shape[0]
    columns = wide_refs[0].shape[0]
    row = lax.broadcasted_iota(jnp.int32, (time_steps, columns), 0)
    col = lax.broadcasted_iota(jnp.int32, (time_steps, columns), 1)
    expand = jnp.where(row == col // 8, 1.0, 0.0).astype(BF16)
    same = (
        lax.broadcasted_iota(jnp.int32, (1, 8, columns), 1)
        == lax.broadcasted_iota(jnp.int32, (1, 8, columns), 2) % 8
    )
    for part, wide_ref in zip(split(noise[...]), wide_refs):
        wide = jnp.dot(part, expand, preferred_element_type=F32)
        wide = jnp.where(same, wide[:, None, :], 0.0)
        wide_ref[...] = wide.reshape(columns, columns).astype(BF16)


def forward_kernel(
    p0, p1, p2, p3, noise, k_high, k_low, out_ref, n_high, n_low, field, f_high, f_low
):
    params, part_columns = p0.shape
    columns = out_ref.shape[0]
    block_rows = GROUP * params
    step_rows = 8 * GROUP
    me = lax.axis_index("sens")
    field[pl.ds(0, step_rows), :] = jnp.zeros((step_rows, params), F32)
    for other, piece in enumerate((p0, p1, p2, p3)):
        start = step_rows + part_columns * jnp.bitwise_xor(me, other)
        field[pl.ds(pl.multiple_of(start, step_rows), part_columns), :] = piece[...].T
    shifted = jnp.concatenate(
        [field[pl.ds(step_rows - 8 * lag, columns), :] for lag in range(GROUP)], axis=1
    )
    f_high[...], f_low[...] = split(shifted)
    widen_noise(noise, (n_high, n_low))
    for b in range(k_high.shape[0] // block_rows):
        rows = pl.ds(b * block_rows, block_rows)
        source = pl.ds(0, columns - step_rows * b)
        target = pl.ds(step_rows * b, columns - step_rows * b)
        both = jnp.concatenate([f_high[source, :], f_low[source, :]], axis=0)
        both = jnp.dot(both, k_high[rows, :], preferred_element_type=F32)
        term = both[: source.size] + both[source.size :]
        term += jnp.dot(f_high[source, :], k_low[rows, :], preferred_element_type=F32)
        if b == 0:
            out_ref[target, :] = term
        else:
            out_ref[target, :] += term


def share_kernel(pieces, k_high, k_low, out_ref):
    del k_high, k_low
    total = jnp.sum(pieces[...], axis=0)
    for part in range(out_ref.shape[0]):
        out_ref[part] = total


def backward_kernel(
    observed, n_high, n_low, sensor_weight, k_high, k_low, kept, sent,
    spread, w_high, w_low, o_high, o_low,
):
    columns, sensors = observed.shape
    params = kept.shape[1]
    part_columns = kept.shape[2]
    block_rows = GROUP * params
    step_rows = 8 * GROUP
    o_high[...], o_low[...] = split(observed[...])
    for start in range(0, columns, NOISE_ROWS):
        rows = pl.ds(start, NOISE_ROWS)
        mixed = jnp.dot(n_high[rows, :], o_high[...], preferred_element_type=F32)
        mixed += jnp.dot(n_high[rows, :], o_low[...], preferred_element_type=F32)
        mixed += jnp.dot(n_low[rows, :], o_high[...], preferred_element_type=F32)
        w_high[rows, :], w_low[rows, :] = split(mixed * sensor_weight[...])
    spread[pl.ds(columns, step_rows), :] = jnp.zeros((step_rows, block_rows), F32)
    for b in range(k_high.shape[0] // block_rows):
        rows = pl.ds(b * block_rows, block_rows)
        source = pl.ds(step_rows * b, columns - step_rows * b)
        target = pl.ds(0, columns - step_rows * b)
        both = jnp.concatenate([w_high[source, :], w_low[source, :]], axis=0)
        both = transposed_dot(both, k_high[rows, :])
        term = both[: source.size] + both[source.size :]
        term += transposed_dot(w_high[source, :], k_low[rows, :])
        if b == 0:
            spread[target, :] = term
        else:
            spread[target, :] += term

    me = lax.axis_index("sens")
    for other, target in enumerate((kept.at[0], sent.at[0], kept.at[1], sent.at[1])):
        start = pl.multiple_of(part_columns * jnp.bitwise_xor(me, other), part_columns)
        total = spread[pl.ds(start, part_columns), pl.ds(0, params)]
        for lag in range(1, GROUP):
            total += spread[pl.ds(start + 8 * lag, part_columns), pl.ds(lag * params, params)]
        target[...] = total.T


def per_device(probes, kernel, noise_inverse, sensor_weight):
    time_steps, params, sensors = kernel.shape
    part_columns = probes.shape[1]
    ranks = lax.axis_size("sens")
    columns = part_columns * ranks
    block_rows = GROUP * params
    par = lax.axis_size("par")
    swap_core = [(s, s ^ 1) for s in range(ranks)]
    swap_chip = [(s, s ^ 2) for s in range(ranks)]
    kernel_rows = time_steps * params
    vmem = pl.BlockSpec(memory_space=pltpu.VMEM)
    hbm = pl.BlockSpec(memory_space=pltpu.HBM)
    compiler_params = pltpu.CompilerParams(vmem_limit_bytes=24 * 1024 * 1024)
    step_rows = 8 * GROUP

    across = lax.ppermute(probes, "sens", swap_chip)
    beside = lax.ppermute(probes, "sens", swap_core)

    half_kernel = jax.ShapeDtypeStruct((kernel_rows, sensors), BF16)
    half_noise = jax.ShapeDtypeStruct((columns, columns), BF16)
    k_high, k_low = pl.pallas_call(
        prepare_kernel,
        out_shape=(half_kernel, half_kernel),
        in_specs=[hbm],
        out_specs=(vmem, vmem),
        scratch_shapes=[
            pltpu.VMEM((kernel_rows, sensors), F32),
            pltpu.SemaphoreType.DMA((PIECES,)),
        ],
        compiler_params=pltpu.CompilerParams(vmem_limit_bytes=40 * 1024 * 1024),
        cost_estimate=pl.CostEstimate(
            flops=8 * kernel_rows * sensors,
            bytes_accessed=8 * kernel_rows * sensors,
            transcendentals=0,
        ),
        name="prepare",
    )(kernel.reshape(kernel_rows, sensors))

    across, k_high = lax.optimization_barrier((across, k_high))
    diagonal = lax.ppermute(across, "sens", swap_core)

    partial, n_high, n_low = pl.pallas_call(
        forward_kernel,
        out_shape=(
            jax.ShapeDtypeStruct((columns, sensors), F32),
            half_noise,
            half_noise,
        ),
        in_specs=[vmem] * 7,
        out_specs=(vmem,) * 3,
        scratch_shapes=[
            pltpu.VMEM((step_rows + columns, params), F32),
            pltpu.VMEM((columns, block_rows), BF16),
            pltpu.VMEM((columns, block_rows), BF16),
        ],
        compiler_params=compiler_params,
        name="forward_map",
    )(probes, beside, across, diagonal, noise_inverse, k_high, k_low)

    pieces = lax.all_to_all(
        partial.reshape(par, columns // par, sensors), "par", 0, 0, tiled=True
    )
    shares = pl.pallas_call(
        share_kernel,
        out_shape=jax.ShapeDtypeStruct(pieces.shape, F32),
        in_specs=[vmem] * 3,
        out_specs=vmem,
        compiler_params=compiler_params,
        name="share",
    )(pieces, k_high, k_low)
    observed = lax.all_to_all(shares, "par", 0, 0, tiled=True).reshape(columns, sensors)

    piece = jax.ShapeDtypeStruct((2, params, part_columns), F32)
    kept, sent = pl.pallas_call(
        backward_kernel,
        out_shape=(piece, piece),
        in_specs=[vmem] * 6,
        out_specs=(vmem, vmem),
        scratch_shapes=[
            pltpu.VMEM((columns + step_rows, block_rows), F32),
            pltpu.VMEM((columns, sensors), BF16),
            pltpu.VMEM((columns, sensors), BF16),
            pltpu.VMEM((columns, sensors), BF16),
            pltpu.VMEM((columns, sensors), BF16),
        ],
        compiler_params=compiler_params,
        name="backward_map",
    )(observed, n_high, n_low, sensor_weight.reshape(1, sensors), k_high, k_low)
    kept += lax.ppermute(sent, "sens", swap_core)
    return kept[0] + lax.ppermute(kept[1], "sens", swap_chip)


def solution(mesh):
    placed = (P("par", "sens"), P(None, "par", "sens"), P(), P("sens"))
    return jax.shard_map(
        per_device, mesh=mesh, in_specs=placed, out_specs=P("par", "sens"), check_vma=False
    )
```

```python
import jax
import jax.numpy as jnp
from jax import lax
from jax.experimental import pallas as pl
from jax.experimental.pallas import tpu as pltpu
from jax.sharding import PartitionSpec as P

F32 = jnp.float32
BF16 = jnp.bfloat16
GROUP = 4
PIECES = 8


def split(value):
    high = value.astype(BF16)
    return high, (value - high.astype(F32)).astype(BF16)


def transposed_dot(left, right):
    return lax.dot_general(left, right, (((1,), (1,)), ((), ())), preferred_element_type=F32)


def prepare_kernel(kernel_ref, k_high, k_low, held, sems):
    blocks = sems.shape[0]
    block_rows = held.shape[0] // blocks

    def block_copy(b):
        rows = pl.ds(pl.multiple_of(b * block_rows, block_rows), block_rows)
        return rows, pltpu.make_async_copy(kernel_ref.at[rows], held.at[rows], sems.at[b])

    for b in range(blocks):
        block_copy(b)[1].start()

    @pl.loop(0, blocks)
    def _(b):
        rows, copy = block_copy(b)
        copy.wait()
        high, low = split(held[rows, :])
        k_high[rows, :] = high
        k_low[rows, :] = low


def forward_kernel(
    p0, p1, p2, p3, k_high, k_low, out_ref, field, f_high, f_low, sums
):
    params, part_columns = p0.shape
    blocks, columns, width = sums.shape
    block_rows = GROUP * params
    step_rows = 8 * GROUP
    me = lax.axis_index("sens")
    field[pl.ds(0, step_rows), :] = jnp.zeros((step_rows, params), F32)
    for other, piece in enumerate((p0, p1, p2, p3)):
        start = step_rows + part_columns * jnp.bitwise_xor(me, other)
        field[pl.ds(pl.multiple_of(start, step_rows), part_columns), :] = piece[...].T
    shifted = jnp.concatenate(
        [field[pl.ds(step_rows - 8 * lag, columns), :] for lag in range(GROUP)], axis=1
    )
    f_high[...], f_low[...] = split(shifted)
    for b in range(k_high.shape[0] // block_rows):
        rows = pl.ds(b * block_rows, block_rows)
        source = pl.ds(0, columns - step_rows * b)
        target = pl.ds(step_rows * b, columns - step_rows * b)
        both = jnp.concatenate([f_high[source, :], f_low[source, :]], axis=0)
        both = jnp.dot(both, k_high[rows, :], preferred_element_type=F32)
        term = both[: source.size] + both[source.size :]
        term += jnp.dot(f_high[source, :], k_low[rows, :], preferred_element_type=F32)
        for block in range(blocks):
            part = term[:, block * width : (block + 1) * width]
            if b == 0:
                sums[block, target, :] = part
            else:
                sums[block, target, :] += part


    for part, place in parts_of(out_ref):
        out_ref[part] = sums[place]


def parts_of(pieces):
    count, time_steps, _ = pieces.shape
    for part in range(count):
        probe, block = divmod(part, count // 8)
        yield part, (block, pl.ds(probe, time_steps, stride=8), slice(None))


def share_kernel(pieces, noise, sensor_weight, k_high, k_low, out_ref):
    del k_high, k_low
    count, _, width = pieces.shape
    high, low = split(jnp.sum(pieces[...], axis=0))
    n_high, n_low = split(noise[...])
    mixed = jnp.dot(n_high, high, preferred_element_type=F32)
    mixed += jnp.dot(n_high, low, preferred_element_type=F32)
    mixed += jnp.dot(n_low, high, preferred_element_type=F32)
    block = lax.rem(lax.axis_index("par"), count // 8)
    mixed *= sensor_weight[:, pl.ds(pl.multiple_of(block * width, width), width)]
    for part in range(count):
        out_ref[part] = mixed


def backward_kernel(pieces, k_high, k_low, kept, sent, whole, spread, w_high, w_low):
    blocks, columns, width = whole.shape
    params = kept.shape[1]
    part_columns = kept.shape[2]
    block_rows = GROUP * params
    step_rows = 8 * GROUP
    for part, place in parts_of(pieces):
        whole[place] = pieces[part]
    for block in range(blocks):
        lanes = pl.ds(block * width, width)
        w_high[:, lanes], w_low[:, lanes] = split(whole[block])
    spread[pl.ds(columns, step_rows), :] = jnp.zeros((step_rows, block_rows), F32)
    for b in range(k_high.shape[0] // block_rows):
        rows = pl.ds(b * block_rows, block_rows)
        source = pl.ds(step_rows * b, columns - step_rows * b)
        target = pl.ds(0, columns - step_rows * b)
        both = jnp.concatenate([w_high[source, :], w_low[source, :]], axis=0)
        both = transposed_dot(both, k_high[rows, :])
        term = both[: source.size] + both[source.size :]
        term += transposed_dot(w_high[source, :], k_low[rows, :])
        if b == 0:
            spread[target, :] = term
        else:
            spread[target, :] += term

    me = lax.axis_index("sens")
    for other, target in enumerate((kept.at[0], sent.at[0], kept.at[1], sent.at[1])):
        start = pl.multiple_of(part_columns * jnp.bitwise_xor(me, other), part_columns)
        total = spread[pl.ds(start, part_columns), pl.ds(0, params)]
        for lag in range(1, GROUP):
            total += spread[pl.ds(start + 8 * lag, part_columns), pl.ds(lag * params, params)]
        target[...] = total.T


def per_device(probes, kernel, noise_inverse, sensor_weight):
    time_steps, params, sensors = kernel.shape
    part_columns = probes.shape[1]
    ranks = lax.axis_size("sens")
    columns = part_columns * ranks
    block_rows = GROUP * params
    par = lax.axis_size("par")
    swap_core = [(s, s ^ 1) for s in range(ranks)]
    swap_chip = [(s, s ^ 2) for s in range(ranks)]
    kernel_rows = time_steps * params
    vmem = pl.BlockSpec(memory_space=pltpu.VMEM)
    hbm = pl.BlockSpec(memory_space=pltpu.HBM)
    compiler_params = pltpu.CompilerParams(vmem_limit_bytes=24 * 1024 * 1024)
    step_rows = 8 * GROUP

    across = lax.ppermute(probes, "sens", swap_chip)
    beside = lax.ppermute(probes, "sens", swap_core)

    half_kernel = jax.ShapeDtypeStruct((kernel_rows, sensors), BF16)
    k_high, k_low = pl.pallas_call(
        prepare_kernel,
        out_shape=(half_kernel, half_kernel),
        in_specs=[hbm],
        out_specs=(vmem, vmem),
        scratch_shapes=[
            pltpu.VMEM((kernel_rows, sensors), F32),
            pltpu.SemaphoreType.DMA((PIECES,)),
        ],
        compiler_params=pltpu.CompilerParams(vmem_limit_bytes=40 * 1024 * 1024),
        cost_estimate=pl.CostEstimate(
            flops=8 * kernel_rows * sensors,
            bytes_accessed=8 * kernel_rows * sensors,
            transcendentals=0,
        ),
        name="prepare",
    )(kernel.reshape(kernel_rows, sensors))

    across, k_high = lax.optimization_barrier((across, k_high))
    diagonal = lax.ppermute(across, "sens", swap_core)

    blocks = par // 8
    shape = jax.ShapeDtypeStruct((par, time_steps, sensors // blocks), F32)
    partial = pl.pallas_call(
        forward_kernel,
        out_shape=shape,
        in_specs=[vmem] * 6,
        out_specs=vmem,
        scratch_shapes=[
            pltpu.VMEM((step_rows + columns, params), F32),
            pltpu.VMEM((columns, block_rows), BF16),
            pltpu.VMEM((columns, block_rows), BF16),
            pltpu.VMEM((blocks, columns, sensors // blocks), F32),
        ],
        compiler_params=compiler_params,
        name="forward_map",
    )(probes, beside, across, diagonal, k_high, k_low)

    pieces = lax.all_to_all(partial, "par", 0, 0, tiled=True)
    shares = pl.pallas_call(
        share_kernel,
        out_shape=shape,
        in_specs=[vmem] * 5,
        out_specs=vmem,
        compiler_params=compiler_params,
        name="share",
    )(pieces, noise_inverse, sensor_weight.reshape(1, sensors), k_high, k_low)
    weighted = lax.all_to_all(shares, "par", 0, 0, tiled=True)

    piece = jax.ShapeDtypeStruct((2, params, part_columns), F32)
    kept, sent = pl.pallas_call(
        backward_kernel,
        out_shape=(piece, piece),
        in_specs=[vmem] * 3,
        out_specs=(vmem, vmem),
        scratch_shapes=[
            pltpu.VMEM((blocks, columns, sensors // blocks), F32),
            pltpu.VMEM((columns + step_rows, block_rows), F32),
            pltpu.VMEM((columns, sensors), BF16),
            pltpu.VMEM((columns, sensors), BF16),
        ],
        compiler_params=compiler_params,
        name="backward_map",
    )(weighted, k_high, k_low)
    kept += lax.ppermute(sent, "sens", swap_core)
    return kept[0] + lax.ppermute(kept[1], "sens", swap_chip)


def solution(mesh):
    placed = (P("par", "sens"), P(None, "par", "sens"), P(), P("sens"))
    return jax.shard_map(
        per_device, mesh=mesh, in_specs=placed, out_specs=P("par", "sens"), check_vma=False
    )
```

```python
import jax
import jax.numpy as jnp
from jax import lax
from jax.experimental import pallas as pl
from jax.experimental.pallas import tpu as pltpu
from jax.sharding import PartitionSpec as P

F32 = jnp.float32
BF16 = jnp.bfloat16
GROUP = 4
PIECES = 8


def split(value):
    high = value.astype(BF16)
    return high, (value - high.astype(F32)).astype(BF16)


def transposed_dot(left, right):
    return lax.dot_general(left, right, (((1,), (1,)), ((), ())), preferred_element_type=F32)


def prepare_kernel(kernel_ref, k_high, k_low, held, sems):
    blocks = sems.shape[0]
    block_rows = held.shape[0] // blocks

    def block_copy(b):
        rows = pl.ds(pl.multiple_of(b * block_rows, block_rows), block_rows)
        return rows, pltpu.make_async_copy(kernel_ref.at[rows], held.at[rows], sems.at[b])

    for b in range(blocks):
        block_copy(b)[1].start()

    @pl.loop(0, blocks)
    def _(b):
        rows, copy = block_copy(b)
        copy.wait()
        high, low = split(held[rows, :])
        k_high[rows, :] = high
        k_low[rows, :] = low


def forward_kernel(
    p0, p1, p2, p3, k_high, k_low, out_ref, field, f_high, f_low, sums
):
    params, part_columns = p0.shape
    blocks, columns, width = sums.shape
    block_rows = GROUP * params
    step_rows = 8 * GROUP
    me = lax.axis_index("sens")
    field[pl.ds(0, step_rows), :] = jnp.zeros((step_rows, params), F32)
    for other, piece in enumerate((p0, p1, p2, p3)):
        start = step_rows + part_columns * jnp.bitwise_xor(me, other)
        field[pl.ds(pl.multiple_of(start, step_rows), part_columns), :] = piece[...].T
    shifted = jnp.concatenate(
        [field[pl.ds(step_rows - 8 * lag, columns), :] for lag in range(GROUP)], axis=1
    )
    f_high[...], f_low[...] = split(shifted)
    for b in range(k_high.shape[0] // block_rows):
        rows = pl.ds(b * block_rows, block_rows)
        source = pl.ds(0, columns - step_rows * b)
        target = pl.ds(step_rows * b, columns - step_rows * b)
        both = jnp.concatenate([f_high[source, :], f_low[source, :]], axis=0)
        both = jnp.dot(both, k_high[rows, :], preferred_element_type=F32)
        term = both[: source.size] + both[source.size :]
        term += jnp.dot(f_high[source, :], k_low[rows, :], preferred_element_type=F32)
        for block in range(blocks):
            part = term[:, block * width : (block + 1) * width]
            if b == 0:
                sums[block, target, :] = part
            else:
                sums[block, target, :] += part


    for part, place in parts_of(out_ref):
        out_ref[part] = sums[place]


def parts_of(pieces):
    count, time_steps, _ = pieces.shape
    for part in range(count):
        probe, block = divmod(part, count // 8)
        yield part, (block, pl.ds(probe, time_steps, stride=8), slice(None))


def share_kernel(pieces, noise, sensor_weight, k_high, k_low, out_ref):
    del k_high, k_low
    count, _, width = pieces.shape
    high, low = split(jnp.sum(pieces[...], axis=0))
    n_high, n_low = split(noise[...])
    mixed = jnp.dot(n_high, high, preferred_element_type=F32)
    mixed += jnp.dot(n_high, low, preferred_element_type=F32)
    mixed += jnp.dot(n_low, high, preferred_element_type=F32)
    block = lax.rem(lax.axis_index("par"), count // 8)
    mixed *= sensor_weight[:, pl.ds(pl.multiple_of(block * width, width), width)]
    for part in range(count):
        out_ref[part] = mixed


def backward_kernel(
    pieces, k_high, k_low, kept, sent, kept_far, sent_far, whole, spread, w_high, w_low
):
    blocks, columns, width = whole.shape
    params, part_columns = kept.shape
    block_rows = GROUP * params
    step_rows = 8 * GROUP
    for part, place in parts_of(pieces):
        whole[place] = pieces[part]
    for block in range(blocks):
        lanes = pl.ds(block * width, width)
        w_high[:, lanes], w_low[:, lanes] = split(whole[block])
    spread[pl.ds(columns, step_rows), :] = jnp.zeros((step_rows, block_rows), F32)
    for b in range(k_high.shape[0] // block_rows):
        rows = pl.ds(b * block_rows, block_rows)
        source = pl.ds(step_rows * b, columns - step_rows * b)
        target = pl.ds(0, columns - step_rows * b)
        both = jnp.concatenate([w_high[source, :], w_low[source, :]], axis=0)
        both = transposed_dot(both, k_high[rows, :])
        term = both[: source.size] + both[source.size :]
        term += transposed_dot(w_high[source, :], k_low[rows, :])
        if b == 0:
            spread[target, :] = term
        else:
            spread[target, :] += term

    me = lax.axis_index("sens")
    for other, target in enumerate((kept, sent, kept_far, sent_far)):
        start = pl.multiple_of(part_columns * jnp.bitwise_xor(me, other), part_columns)
        total = spread[pl.ds(start, part_columns), pl.ds(0, params)]
        for lag in range(1, GROUP):
            total += spread[pl.ds(start + 8 * lag, part_columns), pl.ds(lag * params, params)]
        target[...] = total.T


def per_device(probes, kernel, noise_inverse, sensor_weight):
    time_steps, params, sensors = kernel.shape
    part_columns = probes.shape[1]
    ranks = lax.axis_size("sens")
    columns = part_columns * ranks
    block_rows = GROUP * params
    par = lax.axis_size("par")
    swap_core = [(s, s ^ 1) for s in range(ranks)]
    swap_chip = [(s, s ^ 2) for s in range(ranks)]
    kernel_rows = time_steps * params
    vmem = pl.BlockSpec(memory_space=pltpu.VMEM)
    hbm = pl.BlockSpec(memory_space=pltpu.HBM)
    compiler_params = pltpu.CompilerParams(vmem_limit_bytes=24 * 1024 * 1024)
    step_rows = 8 * GROUP

    across = lax.ppermute(probes, "sens", swap_chip)
    beside = lax.ppermute(probes, "sens", swap_core)

    half_kernel = jax.ShapeDtypeStruct((kernel_rows, sensors), BF16)
    k_high, k_low = pl.pallas_call(
        prepare_kernel,
        out_shape=(half_kernel, half_kernel),
        in_specs=[hbm],
        out_specs=(vmem, vmem),
        scratch_shapes=[
            pltpu.VMEM((kernel_rows, sensors), F32),
            pltpu.SemaphoreType.DMA((PIECES,)),
        ],
        compiler_params=pltpu.CompilerParams(vmem_limit_bytes=40 * 1024 * 1024),
        cost_estimate=pl.CostEstimate(
            flops=8 * kernel_rows * sensors,
            bytes_accessed=8 * kernel_rows * sensors,
            transcendentals=0,
        ),
        name="prepare",
    )(kernel.reshape(kernel_rows, sensors))

    across, k_high = lax.optimization_barrier((across, k_high))
    diagonal = lax.ppermute(across, "sens", swap_core)

    blocks = par // 8
    shape = jax.ShapeDtypeStruct((par, time_steps, sensors // blocks), F32)
    partial = pl.pallas_call(
        forward_kernel,
        out_shape=shape,
        in_specs=[vmem] * 6,
        out_specs=vmem,
        scratch_shapes=[
            pltpu.VMEM((step_rows + columns, params), F32),
            pltpu.VMEM((columns, block_rows), BF16),
            pltpu.VMEM((columns, block_rows), BF16),
            pltpu.VMEM((blocks, columns, sensors // blocks), F32),
        ],
        compiler_params=compiler_params,
        name="forward_map",
    )(probes, beside, across, diagonal, k_high, k_low)

    pieces = lax.all_to_all(partial, "par", 0, 0, tiled=True)
    shares = pl.pallas_call(
        share_kernel,
        out_shape=shape,
        in_specs=[vmem] * 5,
        out_specs=vmem,
        compiler_params=compiler_params,
        name="share",
    )(pieces, noise_inverse, sensor_weight.reshape(1, sensors), k_high, k_low)
    weighted = lax.all_to_all(shares, "par", 0, 0, tiled=True)

    piece = jax.ShapeDtypeStruct((params, part_columns), F32)
    kept, sent, kept_far, sent_far = pl.pallas_call(
        backward_kernel,
        out_shape=(piece,) * 4,
        in_specs=[vmem] * 3,
        out_specs=(vmem,) * 4,
        scratch_shapes=[
            pltpu.VMEM((blocks, columns, sensors // blocks), F32),
            pltpu.VMEM((columns + step_rows, block_rows), F32),
            pltpu.VMEM((columns, sensors), BF16),
            pltpu.VMEM((columns, sensors), BF16),
        ],
        compiler_params=compiler_params,
        name="backward_map",
    )(weighted, k_high, k_low)
    far = kept_far + lax.ppermute(sent_far, "sens", swap_core)
    near = lax.ppermute(sent, "sens", swap_core)
    far = lax.ppermute(far, "sens", swap_chip)
    return kept + near + far


def solution(mesh):
    placed = (P("par", "sens"), P(None, "par", "sens"), P(), P("sens"))
    return jax.shard_map(
        per_device, mesh=mesh, in_specs=placed, out_specs=P("par", "sens"), check_vma=False
    )
```
